32 devices in a mesh: rows: 2 (over y), near: 4 (over z), far: 4 (over x, core).
Axes of the slice: x: 2, y: 2, z: 4, core: 2. Of those that a mesh axis runs over, the one named last changes fastest.
Arguments:
- diag_block: float32 [512, 512], replicated, as said below
- history_rows: float32 [512, 24576], P('rows', ('near', 'far'))
- panel_below: float32 [2048, 512], P(('rows', 'near', 'far')), may hold values from -6 to 6
- history_below: float32 [2048, 24576], P('rows', ('near', 'far')), may hold values from -6 to 6
Outputs:
- panel_factor: float32 [2048, 512], P(('rows', 'near', 'far'))
- diag_factor: float32 [512, 512], replicated
The draws below stay inside these ranges and needn't reach their ends.
Inputs may be any that keep to these rules, and one draw needn't show every extreme that they name: diag_block minus history_rows history_rows^T is symmetric with a dominant positive diagonal.
All inputs are finite; a program needn't handle non-finite values.
Results may differ from the reference program's by a relative error of at most 0.000067.
Values sent between devices are 32-bit elements; how exact they have to be, the bound alone decides.
A program may use at most 64 MiB of HBM per device.

```python
import math
import jax
import jax.numpy as jnp
from jax import lax

PANEL = 512
ROWS_ALL = 2048
HIST = 24576


def history_draw(key):
    base = jax.random.normal(key, (PANEL, HIST), jnp.float32)
    return base / math.sqrt(HIST)


def draw_history_rows(key, part):
    return history_draw(key)


def draw_diag_block(key, part):
    shared = history_draw(key)
    key = jax.random.fold_in(key, 7)
    key_off, key_diag = jax.random.split(key)
    product = jnp.dot(shared, shared.T, precision=lax.Precision.HIGHEST)
    off = jax.random.uniform(key_off, (PANEL, PANEL), jnp.float32, -1.0, 1.0) / PANEL
    off = off + off.T
    diagonal = jax.random.uniform(key_diag, (PANEL,), jnp.float32, 1.5, 3.0)
    return product + off * (1.0 - jnp.eye(PANEL, dtype=jnp.float32)) + jnp.diag(diagonal)


def with_spikes(array, rng, source, target, parts, factor):
    owner, partner = [(jnp.arange(array.shape[axis_at]) // (array.shape[axis_at] // parts)).reshape([-1 if axis == axis_at else 1 for axis in range(array.ndim)]) for axis_at in (source, target)]
    chosen = jax.random.permutation(rng, parts)[partner]
    strong = (owner == chosen) | (owner == (partner + parts // 2) % parts)
    return jnp.where(strong, factor * array, array)


def block_scale(own_key, shape, cuts, smallest, top_value):
    factor_of, own = 1.0, jax.random.fold_in(own_key, 6)
    for axis_at, parts in cuts:
        draws = jnp.exp(jax.random.uniform(jax.random.fold_in(own, axis_at), (parts,), jnp.float32, smallest / len(cuts), top_value / len(cuts)))
        factor_of = factor_of * jnp.repeat(draws, shape[axis_at] // parts).reshape([-1 if axis == axis_at else 1 for axis in range(len(shape))])
    return factor_of


def scatter_about(stream_key, dims, width, limit, cuts=(), held_as=jnp.bfloat16):
    array = jax.random.normal(stream_key, dims, jnp.float32) * width
    if len(cuts) > 0:
        array = block_scale(stream_key, dims, cuts, -0.22, 0.18) * array
    return jnp.clip(array, min=-limit, max=limit).astype(held_as)


def noise_with(stream_key, shape, scale, bound, pieces, heavy, kind=jnp.bfloat16):
    array = scale * jax.random.normal(stream_key, shape, jnp.float32)
    if pieces:
        array = array * block_scale(stream_key, shape, pieces, -0.22, 0.18)
    return jnp.clip(with_spikes(array, jax.random.fold_in(stream_key, 3), *heavy), -bound, bound).astype(kind)


def setup_inputs(seed: int = 0) -> dict:
    arg_keys = jax.random.split(jax.random.key(seed), 5)
    diag_block = draw_diag_block(jax.random.fold_in(arg_keys[4], 71), 0)
    history_rows = draw_history_rows(jax.random.fold_in(arg_keys[4], 71), 0)
    panel_below = scatter_about(arg_keys[2], (ROWS_ALL, PANEL), 1.0, 6.0, ((0, 32),), jnp.float32)
    history_below = noise_with(arg_keys[3], (ROWS_ALL, HIST), 1.0, 6.0, ((0, 2), (1, 16)), (1, 0, 16, 2.0), jnp.float32)
    return dict(diag_block=diag_block, history_rows=history_rows, panel_below=panel_below, history_below=history_below)


def reference(diag_block, history_rows, panel_below, history_below):
    highest = lax.Precision.HIGHEST
    schur = diag_block - jnp.dot(history_rows, history_rows.T, precision=highest)
    diag_factor = jnp.linalg.cholesky(schur)
    identity = jnp.eye(PANEL, dtype=jnp.float32)
    inverse = lax.linalg.triangular_solve(diag_factor, identity, left_side=True, lower=True)
    updated = panel_below - jnp.dot(history_below, history_rows.T, precision=highest)
    panel_factor = jnp.dot(updated, inverse.T, precision=highest)
    return (panel_factor, diag_factor)
```

```python
import jax
import jax.numpy as jnp
from jax import lax
from jax.experimental import pallas as pl
from jax.experimental.pallas import tpu as pltpu
from jax.sharding import PartitionSpec as P

NT = (((1,), (1,)), ((), ()))
NN = (((1,), (0,)), ((), ()))
LIMIT = 5e-5
MAX_STEPS = 12


def split(value):
    high = value.astype(jnp.bfloat16)
    low = (value - high.astype(jnp.float32)).astype(jnp.bfloat16)
    return high, low


def dot3(left, right, dims):
    lh, ll = left
    rh, rl = right
    out = lax.dot_general(lh, rl, dims, preferred_element_type=jnp.float32)
    out += lax.dot_general(ll, rh, dims, preferred_element_type=jnp.float32)
    return out + lax.dot_general(lh, rh, dims, preferred_element_type=jnp.float32)


def norm2(value):
    return jnp.sum(value * value)


def factor_kernel(diag_ref, prod_ref, below_ref, rows_ref, factor_ref, panel_ref, flag_ref,
                  full_ref, m_ref, y_ref):
    size = diag_ref.shape[0]
    row = lax.broadcasted_iota(jnp.int32, (size, size), 0)
    col = lax.broadcasted_iota(jnp.int32, (size, size), 1)
    schur = diag_ref[...] - prod_ref[...]
    on_diag = jnp.where(row == col, schur, 0.0)
    d_col = jnp.sum(on_diag, axis=1, keepdims=True)
    d_row = jnp.sum(on_diag, axis=0, keepdims=True)

    def inv_sqrt(d):
        s = lax.rsqrt(d)
        return s * (1.5 - 0.5 * d * s * s)

    s_col, s_row = inv_sqrt(d_col), inv_sqrt(d_row)
    scaled = jnp.where(row == col, 1.0, schur * s_col * s_row)
    full_ref[...] = scaled
    m_ref[...] = jnp.where(row >= col, scaled, 0.0)
    y_ref[...] = jnp.where(row > col, -scaled, jnp.where(row == col, 1.0, 0.0))

    def step(carry):
        count, _ = carry
        m = m_ref[...]
        m_s = split(m)
        y = y_ref[...]
        y_s = split(y)
        resid = full_ref[...] - dot3(m_s, m_s, NT)
        half = dot3(y_s, split(resid), NN)
        err = dot3(split(half), y_s, NT)
        p = jnp.where(row > col, err, jnp.where(row == col, 0.5 * err, 0.0))
        m = m + dot3(m_s, split(p), NN)
        m_ref[...] = m
        gap = jnp.where(row == col, 1.0, 0.0) - dot3(y_s, split(m), NN)
        y_ref[...] = y + dot3(split(gap), y_s, NN)
        p2, g2 = norm2(p), norm2(gap)
        return count + 1, p2 + g2

    count, left = lax.while_loop(
        lambda c: (c[0] < MAX_STEPS) & (c[1] > LIMIT), step, (jnp.int32(0), jnp.float32(1.0))
    )
    flag_ref[0, 0] = jnp.where(left <= LIMIT, 1, 0).astype(jnp.int32)
    factor_ref[...] = m_ref[...] * (d_col * s_col)
    updated = (below_ref[...] - rows_ref[...]) * s_row
    panel_ref[...] = dot3(split(updated), split(y_ref[...]), NT)


def factor_and_panel(diag_block, products, panel_below, product_rows):
    size = diag_block.shape[0]
    vmem = pl.BlockSpec(memory_space=pltpu.VMEM)
    diag_factor, panel, flag = pl.pallas_call(
        factor_kernel,
        out_shape=(
            jax.ShapeDtypeStruct((size, size), jnp.float32),
            jax.ShapeDtypeStruct(panel_below.shape, jnp.float32),
            jax.ShapeDtypeStruct((1, 1), jnp.int32),
        ),
        in_specs=[vmem] * 4,
        out_specs=(vmem, vmem, pl.BlockSpec(memory_space=pltpu.SMEM)),
        scratch_shapes=[pltpu.VMEM((size, size), jnp.float32)] * 3,
        compiler_params=pltpu.CompilerParams(vmem_limit_bytes=40 * 1024 * 1024),
    )(diag_block, products, panel_below, product_rows)

    def direct():
        schur = diag_block - products
        factor = jnp.linalg.cholesky(schur)
        identity = jnp.eye(size, dtype=jnp.float32)
        inverse = lax.linalg.triangular_solve(factor, identity, left_side=True, lower=True)
        updated = panel_below - product_rows
        return jnp.dot(updated, inverse.T, precision=lax.Precision.HIGHEST), factor

    return lax.cond(flag[0, 0] == 1, lambda: (panel, diag_factor), direct)


def exchange_kernel(hist_ref, below_ref, schur_ref, rows_ref,
                    hist, other, below, below_hi, below_lo, sums, from_core, from_x, from_z,
                    own_all, other_all, local_sem, hist_sem, core_sem, x_sem, z_sem, gather_sem):
    r, z, far = lax.axis_index("rows"), lax.axis_index("near"), lax.axis_index("far")
    x, c = far // 2, lax.rem(far, 2)
    to_y = {"rows": 1 - r}
    to_core = {"far": x * 2 + (1 - c)}
    to_x = {"far": (1 - x) * 2 + c}
    to_z = [{"near": lax.rem(z + d, 4)} for d in (1, 2, 3)]
    half, depth = hist_ref.shape
    piece = depth // 2
    width = half // 2
    pending = []

    barrier = pltpu.get_barrier_semaphore()
    for peer in [to_y, to_core, to_x] + to_z:
        pl.semaphore_signal(barrier, inc=1, device_id=peer, device_id_type=pl.DeviceIdType.MESH)
    pl.semaphore_wait(barrier, 6)

    def send(src, dst, sems, at, peer):
        copy = pltpu.make_async_remote_copy(
            src_ref=src, dst_ref=dst, send_sem=sems.at[(0,) + at], recv_sem=sems.at[(1,) + at],
            device_id=peer, device_id_type=pl.DeviceIdType.MESH)
        copy.start()
        pending.append(copy)
        return copy

    def send_hist(block, k):
        at = (pl.ds(block * width, width), pl.ds(k * piece, piece))
        return send(hist_ref.at[at], other.at[at], hist_sem, (block * 2 + k,), to_y)

    hist_copies = [send_hist(0, 0), send_hist(0, 1), send_hist(1, 0)]
    load_hist = pltpu.make_async_copy(hist_ref, hist, local_sem.at[0])
    load_below = pltpu.make_async_copy(below_ref, below, local_sem.at[1])
    load_hist.start()
    load_below.start()

    def multiply_schur(block, right, first, cols):
        left = split(hist[:, cols])
        value = dot3(left, right, NT)
        rows = value.shape[0] // 16
        for i in range(16):
            at = (i % 2, (i // 2) % 2, i // 4)
            part = value[i * rows:(i + 1) * rows]
            sums[block][0][at] = part if first else sums[block][0][at] + part

    def multiply_below(block, right, first, cols):
        tile = below.shape[0] // 4
        rows = tile // 4
        for t in range(4):
            at_rows = pl.ds(t * tile, tile)
            value = dot3((below_hi[at_rows, cols], below_lo[at_rows, cols]), right, NT)
            for i in range(4):
                at = (i % 2, i // 2, t)
                part = value[i * rows:(i + 1) * rows]
                sums[block][1][at] = part if first else sums[block][1][at] + part

    def core_send(block, kind):
        return send(sums[block][kind].at[1 - c], from_core[block][kind], core_sem, (block, kind), to_core)

    def x_send(block, kind, copy):
        copy.wait_recv()
        total = sums[block][kind]
        total[c] = total[c] + from_core[block][kind][...]
        return send(total.at[c, 1 - x], from_x[block][kind], x_sem, (block, kind), to_x)

    def z_send(block, kind, copy):
        copy.wait_recv()
        total = sums[block][kind]
        total[c, x] = total[c, x] + from_x[block][kind][...]
        return [
            send(total.at[c, x, lax.rem(z + d + 1, 4)], from_z[block][kind].at[d], z_sem, (block, kind, d), to_z[d])
            for d in range(3)
        ]

    def z_total(block, kind, copies):
        for copy in copies:
            copy.wait_recv()
        got = from_z[block][kind]
        return (sums[block][kind][c, x, z] + got[0]) + (got[1] + got[2])

    everything = pl.ds(0, depth)
    load_hist.wait()
    own = split(hist[...])
    multiply_schur(0, own, True, everything)
    core_s = core_send(0, 0)
    load_below.wait()
    tile = below.shape[0] // 8
    for t in range(8):
        at_rows = pl.ds(t * tile, tile)
        high, low = split(below[at_rows, :])
        below_hi[at_rows, :] = high
        below_lo[at_rows, :] = low
    multiply_below(0, own, True, everything)
    core_b = core_send(0, 1)
    x_s = x_send(0, 0, core_s)
    x_b = x_send(0, 1, core_b)
    z_s = z_send(0, 0, x_s)
    own_all[c, x, z, r] = z_total(0, 0, z_s)
    y_own = send(own_all.at[c, x, z, r], own_all.at[c, x, z, r], gather_sem, (0, 0), to_y)
    hist_copies.append(send_hist(1, 1))
    z_b = z_send(0, 1, x_b)

    def gather_z(ref, which, copy):
        copy.wait_recv()
        return [send(ref, ref, gather_sem, (which, 1 + d), to_z[d]) for d in range(3)]

    def gather_x(ref, which, copies):
        for copy in copies:
            copy.wait_recv()
        return send(ref, ref, gather_sem, (which, 4), to_x)

    def gather_core(ref, which, copy):
        copy.wait_recv()
        return send(ref, ref, gather_sem, (which, 5), to_core)

    def other_piece(block, k):
        hist_copies[block * 2 + k].wait_recv()
        cols = pl.ds(k * piece, piece)
        return split(other[pl.ds(block * width, width), cols]), cols

    right, cols = other_piece(0, 0)
    multiply_schur(1, right, True, cols)
    multiply_below(1, right, True, cols)
    right, cols = other_piece(0, 1)
    multiply_schur(1, right, False, cols)
    s1 = core_send(1, 0)
    multiply_below(1, right, False, cols)
    b1 = core_send(1, 1)
    gz = gather_z(own_all.at[c, x, z], 0, y_own)
    s1 = x_send(1, 0, s1)
    b1 = x_send(1, 1, b1)
    rows_ref[:, pl.ds(pl.multiple_of(r * half, half), half)] = z_total(0, 1, z_b)
    gx = gather_x(own_all.at[c, x], 0, gz)
    s1 = z_send(1, 0, s1)
    b1 = z_send(1, 1, b1)
    gc = gather_core(own_all.at[c], 0, gx)
    other_all[r, c, x, z, :, 0:width] = z_total(1, 0, s1)
    right, cols = other_piece(1, 0)
    multiply_schur(2, right, True, cols)
    multiply_below(2, right, True, cols)
    rows_ref[:, pl.ds(pl.multiple_of((1 - r) * half, width), width)] = z_total(1, 1, b1)
    gc.wait_recv()
    right, cols = other_piece(1, 1)
    multiply_schur(2, right, False, cols)
    s2 = core_send(2, 0)
    multiply_below(2, right, False, cols)
    b2 = core_send(2, 1)
    s2 = x_send(2, 0, s2)
    b2 = x_send(2, 1, b2)
    s2 = z_send(2, 0, s2)
    other_all[r, c, x, z, :, width:half] = z_total(2, 0, s2)
    y_other = send(other_all.at[r, c, x, z], other_all.at[r, c, x, z], gather_sem, (1, 0), to_y)
    b2 = z_send(2, 1, b2)
    gz = gather_z(other_all.at[1, c, x, z], 1, y_other)
    gx = gather_x(other_all.at[1, c, x], 1, gz)
    gc = gather_core(other_all.at[1, c], 1, gx)
    rows_ref[:, pl.ds(pl.multiple_of((1 - r) * half + width, width), width)] = z_total(2, 1, b2)
    gc.wait_recv()
    rows = half // 16
    for i in range(16):
        at = (i % 2, (i // 2) % 2, i // 4)
        schur_ref[i * rows:(i + 1) * rows, 0:half] = own_all[at + (0,)]
        schur_ref[half + i * rows:half + (i + 1) * rows, half:2 * half] = own_all[at + (1,)]
        schur_ref[half + i * rows:half + (i + 1) * rows, 0:half] = other_all[(1,) + at]
    schur_ref[0:half, half:2 * half] = schur_ref[half:2 * half, 0:half].T
    for copy in pending:
        copy.wait_send()


def exchange(history_rows, history_below):
    half, depth = history_rows.shape
    count = history_below.shape[0]
    f32 = jnp.float32
    widths = (half, half // 2, half // 2)
    kinds = (half // 16, count // 16)

    def blocks(*lead):
        return [[pltpu.VMEM(lead + (rows, w), f32) for rows in kinds] for w in widths]

    return pl.pallas_call(
        exchange_kernel,
        out_shape=(
            jax.ShapeDtypeStruct((2 * half, 2 * half), f32),
            jax.ShapeDtypeStruct((count // 16, 2 * half), f32),
        ),
        in_specs=[pl.BlockSpec(memory_space=pl.ANY)] * 2,
        out_specs=(pl.BlockSpec(memory_space=pltpu.VMEM),) * 2,
        scratch_shapes=[
            pltpu.VMEM((half, depth), f32),
            pltpu.VMEM((half, depth), f32),
            pltpu.VMEM((count, depth), f32),
            pltpu.VMEM((count, depth), jnp.bfloat16),
            pltpu.VMEM((count, depth), jnp.bfloat16),
            blocks(2, 2, 4),
            blocks(2, 4),
            blocks(4),
            blocks(3),
            pltpu.VMEM((2, 2, 4, 2, half // 16, half), f32),
            pltpu.VMEM((2, 2, 2, 4, half // 16, half), f32),
            pltpu.SemaphoreType.DMA((2,)),
            pltpu.SemaphoreType.DMA((2, 4)),
            pltpu.SemaphoreType.DMA((2, 3, 2)),
            pltpu.SemaphoreType.DMA((2, 3, 2)),
            pltpu.SemaphoreType.DMA((2, 3, 2, 3)),
            pltpu.SemaphoreType.DMA((2, 2, 6)),
        ],
        compiler_params=pltpu.CompilerParams(
            collective_id=0, has_side_effects=True, vmem_limit_bytes=52 * 1024 * 1024
        ),
    )(history_rows, history_below)


def body(diag_block, history_rows, panel_below, history_below):
    grid = tuple(lax.axis_size(name) for name in ("rows", "near", "far"))
    if grid == (2, 4, 4):
        products, product_rows = exchange(history_rows, history_below)
        return factor_and_panel(diag_block, products, panel_below, product_rows)
    high = lax.Precision.HIGH
    gathered = lax.all_gather(history_rows, "rows", axis=0, tiled=True)
    schur_rows = jnp.dot(history_rows, gathered.T, precision=high)
    schur_part = lax.psum_scatter(schur_rows, ("near", "far"), scatter_dimension=0, tiled=True)
    products = lax.all_gather(schur_part, ("rows", "near", "far"), axis=0, tiled=True)
    partial_rows = jnp.dot(history_below, gathered.T, precision=high)
    product_rows = lax.psum_scatter(partial_rows, ("near", "far"), scatter_dimension=0, tiled=True)
    return factor_and_panel(diag_block, products, panel_below, product_rows)


def solution(mesh):
    return jax.shard_map(
        body,
        mesh=mesh,
        in_specs=(
            P(),
            P("rows", ("near", "far")),
            P(("rows", "near", "far"), None),
            P("rows", ("near", "far")),
        ),
        out_specs=(P(("rows", "near", "far"), None), P()),
        check_vma=False,
    )
```

```python
import jax
import jax.numpy as jnp
from jax import lax
from jax.experimental import pallas as pl
from jax.experimental.pallas import tpu as pltpu
from jax.sharding import PartitionSpec as P

NT = (((1,), (1,)), ((), ()))
NN = (((1,), (0,)), ((), ()))
LIMIT = 8e-6
VMEM_BYTES = 56 * 1024 * 1024


def split(value):
    high = value.astype(jnp.bfloat16)
    low = (value - high.astype(jnp.float32)).astype(jnp.bfloat16)
    return high, low


def dot1(left, right, dims):
    return lax.dot_general(left, right, dims, preferred_element_type=jnp.float32)


def dot3(left, right, dims):
    lh, ll = left
    rh, rl = right
    return (dot1(lh, rl, dims) + dot1(ll, rh, dims)) + dot1(lh, rh, dims)


def narrow(value):
    return value.astype(jnp.bfloat16)


def norm2(value):
    return jnp.sum(value * value)


def inv_sqrt(d):
    s = lax.rsqrt(d)
    return s * (1.5 - 0.5 * d * s * s)


def grid_of(size):
    row = lax.broadcasted_iota(jnp.int32, (size, size), 0)
    col = lax.broadcasted_iota(jnp.int32, (size, size), 1)
    return row, col


def lower_half(value):
    row, col = grid_of(value.shape[0])
    return jnp.where(row > col, value, jnp.where(row == col, 0.5 * value, 0.0))


def diagonal(value):
    row, col = grid_of(value.shape[0])
    on = jnp.where(row == col, value, 0.0)
    return jnp.sum(on, axis=1, keepdims=True), jnp.sum(on, axis=0, keepdims=True)


def first_step(schur_ref, full_ref, m_ref, y_ref):
    schur = schur_ref[...]
    row, col = grid_of(schur.shape[0])
    d_col, d_row = diagonal(schur)
    scaled = jnp.where(row == col, 1.0, schur * inv_sqrt(d_col) * inv_sqrt(d_row))
    full_ref[...] = scaled
    p0 = jnp.where(row > col, scaled, 0.0)
    identity = jnp.where(row == col, 1.0, 0.0)
    p0b = narrow(p0)
    y0b = narrow(identity - p0)
    resid = -dot1(p0b, p0b, NT)
    p = lower_half(dot1(narrow(dot1(y0b, narrow(resid), NN)), y0b, NT))
    m0 = identity + p0
    q = dot1(narrow(m0), narrow(p), NN)
    m_ref[...] = m0 + q
    gap = dot1(p0b, p0b, NN) - dot1(y0b, narrow(q), NN)
    y_ref[...] = (identity - p0) + dot1(narrow(gap), y0b, NN)


def second_step_factor(full_ref, m_ref, y_ref):
    m = m_ref[...]
    m_s = split(m)
    yb = narrow(y_ref[...])
    resid = full_ref[...] - dot3(m_s, m_s, NT)
    p = lower_half(dot1(narrow(dot1(yb, narrow(resid), NN)), yb, NT))
    m_ref[...] = m + dot1(m_s[0], narrow(p), NN)
    return norm2(p)


def second_step_inverse(m_ref, y_ref):
    y = y_ref[...]
    y_s = split(y)
    row, col = grid_of(y.shape[0])
    gap = jnp.where(row == col, 1.0, 0.0) - dot3(y_s, split(m_ref[...]), NN)
    y_ref[...] = y + dot1(narrow(gap), y_s[0], NN)
    return norm2(gap)


def direct_kernel(left_ref, factor_in, panel_in, schur_ref, rows_ref, factor_ref, panel_ref, work):
    converged = left_ref[0, 0] <= LIMIT
    factor_ref[...] = jnp.where(converged, factor_in[...], 0.0)
    panel_ref[...] = jnp.where(converged, panel_in[...], rows_ref[...])

    @pl.when(jnp.logical_not(converged))
    def _():
        work[...] = schur_ref[...]
        size = work.shape[0]
        row, col = grid_of(size)
        lane = lax.broadcasted_iota(jnp.int32, (1, size), 1)
        line = lax.broadcasted_iota(jnp.int32, (size, 1), 0)

        @pl.loop(0, size)
        def _(j):
            now = work[...]
            here = jnp.sum(jnp.where(row == j, now, 0.0), axis=0, keepdims=True)
            column = jnp.sum(jnp.where(col == j, now, 0.0), axis=1, keepdims=True)
            scale = inv_sqrt(jnp.sum(jnp.where(lane == j, here, 0.0), axis=1, keepdims=True))
            l_col = jnp.where(line >= j, column * scale, 0.0)
            l_row = jnp.where(lane >= j, here * scale, 0.0)
            work[...] = now - l_col * l_row
            factor_ref[...] = jnp.where(col == j, l_col, factor_ref[...])
            rest = panel_ref[...]
            solved = jnp.sum(jnp.where(lane == j, rest, 0.0), axis=1, keepdims=True) * scale
            panel_ref[...] = jnp.where(lane == j, solved, rest - solved * l_row)


def exchange_kernel(hist_ref, below_ref, diag_ref, panel_ref,
                    factor_ref, out_ref, schur_ref, rows_ref, left_ref,
                    hist, other, below, below_hi, below_lo, sums, from_core, from_x, from_z,
                    own_all, other_all, from_y, full, m, y,
                    local_sem, hist_sem, core_sem, x_sem, z_sem, gather_sem):
    r, z, far = lax.axis_index("rows"), lax.axis_index("near"), lax.axis_index("far")
    x, c = far // 2, lax.rem(far, 2)
    to_y = {"rows": 1 - r}
    to_core = {"far": x * 2 + (1 - c)}
    to_x = {"far": (1 - x) * 2 + c}
    to_z = [{"near": lax.rem(z + d, 4)} for d in (1, 2, 3)]
    half, depth = hist_ref.shape
    piece = depth // 2
    width = half // 2
    pending = []

    barrier = pltpu.get_barrier_semaphore()
    for peer in [to_y, to_core, to_x] + to_z:
        pl.semaphore_signal(barrier, inc=1, device_id=peer, device_id_type=pl.DeviceIdType.MESH)
    pl.semaphore_wait(barrier, 6)

    def send(src, dst, sems, at, peer):
        copy = pltpu.make_async_remote_copy(
            src_ref=src, dst_ref=dst, send_sem=sems.at[(0,) + at], recv_sem=sems.at[(1,) + at],
            device_id=peer, device_id_type=pl.DeviceIdType.MESH)
        copy.start()
        pending.append(copy)
        return copy

    def columns(which):
        return pl.ds(pl.multiple_of(which * piece, piece), piece)

    everything = pl.ds(0, depth)
    lines = (pl.ds(0, half), pl.ds(0, width), pl.ds(width, width))

    def send_hist(index):
        at = (lines[index], columns(r if index == 0 else 1 - r))
        return send(hist_ref.at[at], other.at[at], hist_sem, (index,), to_y)

    load_hist = pltpu.make_async_copy(hist_ref, hist, local_sem.at[0])
    load_below = pltpu.make_async_copy(below_ref, below, local_sem.at[1])
    arrive = [send_hist(0), send_hist(1)]
    load_hist.start()
    load_below.start()

    def put_schur(stream, value):
        rows = value.shape[0] // 16
        for i in range(16):
            sums[stream][i % 2, (i // 2) % 2, i // 4] = value[i * rows:(i + 1) * rows]

    def multiply_below(streams, right, first, cols):
        tile = below.shape[0] // 4
        rows = tile // 4
        for t in range(4):
            at_rows = pl.ds(t * tile, tile)
            value = dot3((below_hi[at_rows, cols], below_lo[at_rows, cols]), right, NT)
            for i in range(4):
                at = (i % 2, i // 2, t)
                start = 0
                for stream in streams:
                    wide = sums[stream].shape[-1]
                    part = value[i * rows:(i + 1) * rows, start:start + wide]
                    sums[stream][at] = part if first else sums[stream][at] + part
                    start += wide

    def core_send(stream):
        return send(sums[stream].at[1 - c], from_core[stream], core_sem, (stream,), to_core)

    def x_send(stream, copy):
        copy.wait_recv()
        total = sums[stream]
        total[c] = total[c] + from_core[stream][...]
        return send(total.at[c, 1 - x], from_x[stream], x_sem, (stream,), to_x)

    def z_send(stream, copy):
        copy.wait_recv()
        total = sums[stream]
        total[c, x] = total[c, x] + from_x[stream][...]
        return [
            send(total.at[c, x, lax.rem(z + d + 1, 4)], from_z[stream].at[d], z_sem, (stream, d), to_z[d])
            for d in range(3)
        ]

    def z_total(stream, copies):
        for copy in copies:
            copy.wait_recv()
        got = from_z[stream]
        return (sums[stream][c, x, z] + got[0]) + (got[1] + got[2])

    def gather_z(ref, which):
        return [send(ref, ref, gather_sem, (which, 1 + d), to_z[d]) for d in range(3)]

    def gather_x(ref, which, copies):
        for copy in copies:
            copy.wait_recv()
        return send(ref, ref, gather_sem, (which, 4), to_x)

    def gather_core(ref, which, copy):
        copy.wait_recv()
        return send(ref, ref, gather_sem, (which, 5), to_core)

    def put_rows(stream, copies, start, wide):
        at = (slice(None), pl.ds(pl.multiple_of(start, wide), wide))
        rows_ref[at] = panel_ref[at] - z_total(stream, copies)

    load_hist.wait()
    own = split(hist[...])
    put_schur(0, dot3(own, own, NT))
    s0 = core_send(0)
    load_below.wait()
    tile = below.shape[0] // 8
    for t in range(8):
        at_rows = pl.ds(t * tile, tile)
        high, low = split(below[at_rows, :])
        below_hi[at_rows, :] = high
        below_lo[at_rows, :] = low
    multiply_below((1,), own, True, everything)
    b0 = core_send(1)
    s0 = x_send(0, s0)
    b0 = x_send(1, b0)
    s0 = z_send(0, s0)
    own_all[c, x, z, r] = z_total(0, s0)
    y_own = send(own_all.at[c, x, z, r], own_all.at[c, x, z, r], gather_sem, (0, 0), to_y)
    b0 = z_send(1, b0)

    arrive[0].wait_recv()
    early = columns(1 - r)
    mine, theirs = hist[:, early], other[:, early]
    right = split(theirs)
    put_schur(2, dot3(split(jnp.where(r == 1, mine, theirs)), split(jnp.where(r == 1, theirs, mine)), NT))
    s1 = core_send(2)
    y_own.wait_recv()
    g0 = gather_z(own_all.at[c, x, z], 0)
    s1 = x_send(2, s1)
    g0 = gather_x(own_all.at[c, x], 0, g0)
    s1 = z_send(2, s1)
    g0 = gather_core(own_all.at[c], 0, g0)
    mine = z_total(2, s1)
    other_all[c, x, z] = mine
    y_other = send(other_all.at[c, x, z], from_y, gather_sem, (1, 0), to_y)
    arrive.append(send_hist(2))
    multiply_below((3, 4), right, True, early)
    put_rows(1, b0, r * half, half)
    y_other.wait_recv()
    y_other.wait_send()
    pending[:] = [copy for copy in pending if copy is not y_other]
    other_all[c, x, z] = other_all[c, x, z] + from_y[...]
    g1 = gather_z(other_all.at[c, x, z], 1)
    late = columns(r)
    arrive[1].wait_recv()
    multiply_below((3,), split(other[lines[1], late]), False, late)
    b1 = core_send(3)
    g1 = gather_x(other_all.at[c, x], 1, g1)
    b1 = x_send(3, b1)
    g1 = gather_core(other_all.at[c], 1, g1)
    b1 = z_send(3, b1)

    g0.wait_recv()
    rows = half // 16
    for i in range(16):
        at = (i % 2, (i // 2) % 2, i // 4)
        for group in range(2):
            place = (pl.ds(group * half + i * rows, rows), pl.ds(group * half, half))
            schur_ref[place] = diag_ref[place] - own_all[at + (group,)]
    g1.wait_recv()
    for i in range(16):
        at = (i % 2, (i // 2) % 2, i // 4)
        place = (pl.ds(half + i * rows, rows), pl.ds(0, half))
        schur_ref[place] = diag_ref[place] - other_all[at]
    schur_ref[0:half, half:2 * half] = schur_ref[half:2 * half, 0:half].T
    first_step(schur_ref, full, m, y)

    arrive[2].wait_recv()
    multiply_below((4,), split(other[lines[2], late]), False, late)
    b2 = core_send(4)
    put_rows(3, b1, (1 - r) * half, width)
    left = second_step_factor(full, m, y)
    b2 = x_send(4, b2)
    left += second_step_inverse(m, y)
    left_ref[0, 0] = left
    b2 = z_send(4, b2)
    d_col, d_row = diagonal(schur_ref[...])
    factor_ref[...] = m[...] * (d_col * inv_sqrt(d_col))
    y_s = split(y[...])
    scale = inv_sqrt(d_row)
    put_rows(4, b2, (1 - r) * half + width, width)
    out_ref[...] = dot3(split(rows_ref[...] * scale), y_s, NT)
    for copy in pending:
        copy.wait_send()


def exchange(history_rows, history_below, diag_block, panel_below):
    half, depth = history_rows.shape
    count = history_below.shape[0]
    size = diag_block.shape[0]
    f32 = jnp.float32
    schur_rows, share = half // 16, count // 16
    streams = ((schur_rows, half), (share, half), (schur_rows, half), (share, half // 2), (share, half // 2))

    def blocks(*lead):
        return [pltpu.VMEM(lead + stream, f32) for stream in streams]

    square = jax.ShapeDtypeStruct((size, size), f32)
    strip = jax.ShapeDtypeStruct((share, size), f32)
    vmem = pl.BlockSpec(memory_space=pltpu.VMEM)
    return pl.pallas_call(
        exchange_kernel,
        out_shape=(square, strip, square, strip, jax.ShapeDtypeStruct((1, 1), f32)),
        in_specs=[pl.BlockSpec(memory_space=pl.ANY)] * 2 + [vmem] * 2,
        out_specs=(vmem,) * 4 + (pl.BlockSpec(memory_space=pltpu.SMEM),),
        scratch_shapes=[
            pltpu.VMEM((half, depth), f32),
            pltpu.VMEM((half, depth), f32),
            pltpu.VMEM((count, depth), f32),
            pltpu.VMEM((count, depth), jnp.bfloat16),
            pltpu.VMEM((count, depth), jnp.bfloat16),
            blocks(2, 2, 4),
            blocks(2, 4),
            blocks(4),
            blocks(3),
            pltpu.VMEM((2, 2, 4, 2, schur_rows, half), f32),
            pltpu.VMEM((2, 2, 4, schur_rows, half), f32),
            pltpu.VMEM((schur_rows, half), f32),
            pltpu.VMEM((size, size), f32),
            pltpu.VMEM((size, size), f32),
            pltpu.VMEM((size, size), f32),
            pltpu.SemaphoreType.DMA((2,)),
            pltpu.SemaphoreType.DMA((2, 3)),
            pltpu.SemaphoreType.DMA((2, 5)),
            pltpu.SemaphoreType.DMA((2, 5)),
            pltpu.SemaphoreType.DMA((2, 5, 3)),
            pltpu.SemaphoreType.DMA((2, 2, 6)),
        ],
        compiler_params=pltpu.CompilerParams(
            collective_id=0, has_side_effects=True, vmem_limit_bytes=VMEM_BYTES
        ),
    )(history_rows, history_below, diag_block, panel_below)


def finish(factor, panel, schur, updated, left):
    vmem = pl.BlockSpec(memory_space=pltpu.VMEM)
    factor, panel = pl.pallas_call(
        direct_kernel,
        out_shape=(
            jax.ShapeDtypeStruct(factor.shape, jnp.float32),
            jax.ShapeDtypeStruct(panel.shape, jnp.float32),
        ),
        in_specs=[pl.BlockSpec(memory_space=pltpu.SMEM)] + [vmem] * 4,
        out_specs=(vmem, vmem),
        scratch_shapes=[pltpu.VMEM(factor.shape, jnp.float32)],
        compiler_params=pltpu.CompilerParams(vmem_limit_bytes=VMEM_BYTES),
    )(left, factor, panel, schur, updated)
    return panel, factor


def body(diag_block, history_rows, panel_below, history_below):
    grid = tuple(lax.axis_size(name) for name in ("rows", "near", "far"))
    if grid == (2, 4, 4):
        return finish(*exchange(history_rows, history_below, diag_block, panel_below))
    high = lax.Precision.HIGH
    gathered = lax.all_gather(history_rows, "rows", axis=0, tiled=True)
    schur_rows = jnp.dot(history_rows, gathered.T, precision=high)
    schur_part = lax.psum_scatter(schur_rows, ("near", "far"), scatter_dimension=0, tiled=True)
    products = lax.all_gather(schur_part, ("rows", "near", "far"), axis=0, tiled=True)
    partial_rows = jnp.dot(history_below, gathered.T, precision=high)
    product_rows = lax.psum_scatter(partial_rows, ("near", "far"), scatter_dimension=0, tiled=True)
    schur = diag_block - products
    diag_factor = jnp.linalg.cholesky(schur)
    identity = jnp.eye(schur.shape[0], dtype=jnp.float32)
    inverse = lax.linalg.triangular_solve(diag_factor, identity, left_side=True, lower=True)
    panel_factor = jnp.dot(panel_below - product_rows, inverse.T, precision=high)
    return (panel_factor, diag_factor)


def solution(mesh):
    return jax.shard_map(
        body,
        mesh=mesh,
        in_specs=(
            P(),
            P("rows", ("near", "far")),
            P(("rows", "near", "far"), None),
            P("rows", ("near", "far")),
        ),
        out_specs=(P(("rows", "near", "far"), None), P()),
        check_vma=False,
    )
```

```python
import jax
import jax.numpy as jnp
from jax import lax
from jax.experimental import pallas as pl
from jax.experimental.pallas import tpu as pltpu
from jax.sharding import PartitionSpec as P

NT = (((1,), (1,)), ((), ()))
NN = (((1,), (0,)), ((), ()))
LIMIT = 8e-6
VMEM_BYTES = 56 * 1024 * 1024


def split(value):
    high = value.astype(jnp.bfloat16)
    low = (value - high.astype(jnp.float32)).astype(jnp.bfloat16)
    return high, low


def dot1(left, right, dims):
    return lax.dot_general(left, right, dims, preferred_element_type=jnp.float32)


def dot3(left, right, dims):
    lh, ll = left
    rh, rl = right
    return (dot1(lh, rl, dims) + dot1(ll, rh, dims)) + dot1(lh, rh, dims)


def narrow(value):
    return value.astype(jnp.bfloat16)


def norm2(value):
    return jnp.sum(value * value)


def inv_sqrt(d):
    s = lax.rsqrt(d)
    return s * (1.5 - 0.5 * d * s * s)


def grid_of(size):
    row = lax.broadcasted_iota(jnp.int32, (size, size), 0)
    col = lax.broadcasted_iota(jnp.int32, (size, size), 1)
    return row, col


def lower_half(value):
    row, col = grid_of(value.shape[0])
    return jnp.where(row > col, value, jnp.where(row == col, 0.5 * value, 0.0))


def diagonal(value):
    row, col = grid_of(value.shape[0])
    on = jnp.where(row == col, value, 0.0)
    return jnp.sum(on, axis=1, keepdims=True), jnp.sum(on, axis=0, keepdims=True)


def first_step(schur_ref, full_ref, m_ref, y_ref):
    schur = schur_ref[...]
    row, col = grid_of(schur.shape[0])
    d_col, d_row = diagonal(schur)
    scaled = jnp.where(row == col, 1.0, schur * inv_sqrt(d_col) * inv_sqrt(d_row))
    full_ref[...] = scaled
    p0 = jnp.where(row > col, scaled, 0.0)
    identity = jnp.where(row == col, 1.0, 0.0)
    p0b = narrow(p0)
    y0b = narrow(identity - p0)
    resid = -dot1(p0b, p0b, NT)
    p = lower_half(dot1(narrow(dot1(y0b, narrow(resid), NN)), y0b, NT))
    m0 = identity + p0
    q = dot1(narrow(m0), narrow(p), NN)
    m_ref[...] = m0 + q
    gap = dot1(p0b, p0b, NN) - dot1(y0b, narrow(q), NN)
    y_ref[...] = (identity - p0) + dot1(narrow(gap), y0b, NN)


def second_step_factor(full_ref, m_ref, y_ref):
    m = m_ref[...]
    m_s = split(m)
    yb = narrow(y_ref[...])
    resid = full_ref[...] - dot3(m_s, m_s, NT)
    p = lower_half(dot1(narrow(dot1(yb, narrow(resid), NN)), yb, NT))
    m_ref[...] = m + dot1(m_s[0], narrow(p), NN)
    return norm2(p)


def second_step_inverse(m_ref, y_ref):
    y = y_ref[...]
    y_s = split(y)
    row, col = grid_of(y.shape[0])
    gap = jnp.where(row == col, 1.0, 0.0) - dot3(y_s, split(m_ref[...]), NN)
    y_ref[...] = y + dot1(narrow(gap), y_s[0], NN)
    return norm2(gap)


def direct_kernel(left_ref, factor_in, panel_in, schur_ref, rows_ref, factor_ref, panel_ref, work, factor, rest, sem):
    def move(*pairs):
        copies = [pltpu.make_async_copy(*pair, sem.at[i]) for i, pair in enumerate(pairs)]
        for copy in copies:
            copy.start()
        for copy in copies:
            copy.wait()

    move((factor_in, factor_ref), (panel_in, panel_ref))

    @pl.when(jnp.logical_not(left_ref[0, 0] <= LIMIT))
    def _():
        move((schur_ref, work), (rows_ref, rest))
        factor[...] = jnp.zeros_like(factor)
        size = work.shape[0]
        row, col = grid_of(size)
        lane = lax.broadcasted_iota(jnp.int32, (1, size), 1)
        line = lax.broadcasted_iota(jnp.int32, (size, 1), 0)

        @pl.loop(0, size)
        def _(j):
            now = work[...]
            here = jnp.sum(jnp.where(row == j, now, 0.0), axis=0, keepdims=True)
            column = jnp.sum(jnp.where(col == j, now, 0.0), axis=1, keepdims=True)
            scale = inv_sqrt(jnp.sum(jnp.where(lane == j, here, 0.0), axis=1, keepdims=True))
            l_col = jnp.where(line >= j, column * scale, 0.0)
            l_row = jnp.where(lane >= j, here * scale, 0.0)
            work[...] = now - l_col * l_row
            factor[...] = jnp.where(col == j, l_col, factor[...])
            left = rest[...]
            solved = jnp.sum(jnp.where(lane == j, left, 0.0), axis=1, keepdims=True) * scale
            rest[...] = jnp.where(lane == j, solved, left - solved * l_row)

        move((factor, factor_ref), (rest, panel_ref))


def pack(value):
    rows = value.shape[0] // 2
    return jnp.concatenate([value[:rows], value[rows:]], axis=1)


def unpack(value):
    cols = value.shape[1] // 2
    return jnp.concatenate([value[:, :cols], value[:, cols:]], axis=0)


def exchange_kernel(hist_ref, below_ref, diag_in, panel_in,
                    factor_out, out_ref, schur_out, rows_ref, left_ref,
                    diag_ref, panel_ref, schur_ref, factor_ref, hist, other, below, below_hi, below_lo, sums, from_core, from_x, from_z,
                    own_all, other_all, from_y, full, m, y,
                    local_sem, hist_sem, core_sem, x_sem, z_sem, gather_sem):
    r, z, far = lax.axis_index("rows"), lax.axis_index("near"), lax.axis_index("far")
    x, c = far // 2, lax.rem(far, 2)
    to_y = {"rows": 1 - r}
    to_core = {"far": x * 2 + (1 - c)}
    to_x = {"far": (1 - x) * 2 + c}
    to_z = [{"near": lax.rem(z + d, 4)} for d in (1, 2, 3)]
    half, depth = hist_ref.shape
    piece = depth // 2
    width = half // 2
    pending = []

    barrier = pltpu.get_barrier_semaphore()
    for peer in [to_y, to_core, to_x] + to_z:
        pl.semaphore_signal(barrier, inc=1, device_id=peer, device_id_type=pl.DeviceIdType.MESH)
    pl.semaphore_wait(barrier, 6)

    def send(src, dst, sems, at, peer):
        copy = pltpu.make_async_remote_copy(
            src_ref=src, dst_ref=dst, send_sem=sems.at[(0,) + at], recv_sem=sems.at[(1,) + at],
            device_id=peer, device_id_type=pl.DeviceIdType.MESH)
        copy.start()
        pending.append(copy)
        return copy

    def columns(which):
        return pl.ds(pl.multiple_of(which * piece, piece), piece)

    everything = pl.ds(0, depth)
    quarter = width // 2
    lines = (pl.ds(0, half), pl.ds(0, width), pl.ds(width, quarter), pl.ds(width + quarter, quarter))

    def send_hist(index):
        at = (lines[index], columns(r if index == 0 else 1 - r))
        return send(hist_ref.at[at], other.at[at], hist_sem, (index,), to_y)

    load_hist = pltpu.make_async_copy(hist_ref, hist, local_sem.at[0])
    load_below = pltpu.make_async_copy(below_ref, below, local_sem.at[1])
    load_diag = pltpu.make_async_copy(diag_in, diag_ref, local_sem.at[2])
    load_panel = pltpu.make_async_copy(panel_in, panel_ref, local_sem.at[3])
    arrive = [send_hist(0)]
    load_hist.start()
    load_below.start()
    load_diag.start()
    load_panel.start()

    def put_schur(stream, value):
        rows = value.shape[0] // 16
        for i in range(16):
            sums[stream][i % 2, (i // 2) % 2, i // 4] = value[i * rows:(i + 1) * rows]

    def multiply_below(streams, right, first, cols):
        tile = below.shape[0] // 4
        rows = tile // 4
        for t in range(4):
            at_rows = pl.ds(t * tile, tile)
            value = dot3((below_hi[at_rows, cols], below_lo[at_rows, cols]), right, NT)
            for i in range(4):
                at = (i % 2, i // 2, t)
                start = 0
                for stream in streams:
                    wide = quarter if stream >= 4 else sums[stream].shape[-1]
                    part = value[i * rows:(i + 1) * rows, start:start + wide]
                    if stream >= 4:
                        part = pack(part)
                    sums[stream][at] = part if first else sums[stream][at] + part
                    start += wide

    def core_send(stream):
        return send(sums[stream].at[1 - c], from_core[stream], core_sem, (stream,), to_core)

    def x_send(stream, copy):
        copy.wait_recv()
        total = sums[stream]
        total[c] = total[c] + from_core[stream][...]
        return send(total.at[c, 1 - x], from_x[stream], x_sem, (stream,), to_x)

    def z_send(stream, copy):
        copy.wait_recv()
        total = sums[stream]
        total[c, x] = total[c, x] + from_x[stream][...]
        return [
            send(total.at[c, x, lax.rem(z + d + 1, 4)], from_z[stream].at[d], z_sem, (stream, d), to_z[d])
            for d in range(3)
        ]

    def z_total(stream, copies):
        for copy in copies:
            copy.wait_recv()
        got = from_z[stream]
        return (sums[stream][c, x, z] + got[0]) + (got[1] + got[2])

    def gather_z(ref, which):
        return [send(ref, ref, gather_sem, (which, 1 + d), to_z[d]) for d in range(3)]

    def gather_x(ref, which, copies):
        for copy in copies:
            copy.wait_recv()
        return send(ref, ref, gather_sem, (which, 4), to_x)

    def gather_core(ref, which, copy):
        copy.wait_recv()
        return send(ref, ref, gather_sem, (which, 5), to_core)

    def put_rows(stream, copies, start, wide):
        at = (slice(None), pl.ds(pl.multiple_of(start, wide), wide))
        rows_ref[at] = panel_ref[at] - z_total(stream, copies)

    load_hist.wait()
    own = split(hist[...])
    put_schur(0, dot3(own, own, NT))
    s0 = core_send(0)
    load_below.wait()
    tile = below.shape[0] // 8
    for t in range(8):
        at_rows = pl.ds(t * tile, tile)
        high, low = split(below[at_rows, :])
        below_hi[at_rows, :] = high
        below_lo[at_rows, :] = low
    multiply_below((1,), own, True, everything)
    b0 = core_send(1)
    s0 = x_send(0, s0)
    b0 = x_send(1, b0)
    s0 = z_send(0, s0)
    own_all[c, x, z, r] = z_total(0, s0)
    y_own = send(own_all.at[c, x, z, r], own_all.at[c, x, z, r], gather_sem, (0, 0), to_y)
    arrive.append(send_hist(1))
    b0 = z_send(1, b0)

    arrive[0].wait_recv()
    early, late = columns(1 - r), columns(r)
    mine, theirs = hist[:, early], other[:, early]
    right = split(theirs)
    put_schur(2, dot3(split(jnp.where(r == 1, mine, theirs)), split(jnp.where(r == 1, theirs, mine)), NT))
    s1 = core_send(2)
    s1 = x_send(2, s1)
    s1 = z_send(2, s1)
    other_all[c, x, z] = z_total(2, s1)
    y_other = send(other_all.at[c, x, z], from_y, gather_sem, (1, 0), to_y)
    arrive.append(send_hist(2))
    arrive.append(send_hist(3))
    y_own.wait_recv()
    g0 = gather_z(own_all.at[c, x, z], 0)
    multiply_below((3, 4, 5), right, True, early)
    g0 = gather_x(own_all.at[c, x], 0, g0)
    load_panel.wait()
    put_rows(1, b0, r * half, half)
    g0 = gather_core(own_all.at[c], 0, g0)
    y_other.wait_recv()
    y_other.wait_send()
    pending[:] = [copy for copy in pending if copy is not y_other]
    other_all[c, x, z] = other_all[c, x, z] + from_y[...]
    g1 = gather_z(other_all.at[c, x, z], 1)
    load_diag.wait()
    g0.wait_recv()
    rows = half // 16
    for i in range(16):
        at = (i % 2, (i // 2) % 2, i // 4)
        for group in range(2):
            place = (pl.ds(group * half + i * rows, rows), pl.ds(group * half, half))
            schur_ref[place] = diag_ref[place] - own_all[at + (group,)]
    g1 = gather_x(other_all.at[c, x], 1, g1)
    arrive[1].wait_recv()
    multiply_below((3,), split(other[lines[1], late]), False, late)
    b1 = core_send(3)
    g1 = gather_core(other_all.at[c], 1, g1)
    b1 = x_send(3, b1)
    g1.wait_recv()
    for i in range(16):
        at = (i % 2, (i // 2) % 2, i // 4)
        place = (pl.ds(half + i * rows, rows), pl.ds(0, half))
        schur_ref[place] = diag_ref[place] - other_all[at]
    schur_ref[0:half, half:2 * half] = schur_ref[half:2 * half, 0:half].T
    save_schur = pltpu.make_async_copy(schur_ref, schur_out, local_sem.at[4])
    save_schur.start()
    b1 = z_send(3, b1)
    first_step(schur_ref, full, m, y)

    arrive[2].wait_recv()
    multiply_below((4,), split(other[lines[2], late]), False, late)
    b2 = core_send(4)
    put_rows(3, b1, (1 - r) * half, width)
    left = second_step_factor(full, m, y)
    b2 = x_send(4, b2)
    arrive[3].wait_recv()
    multiply_below((5,), split(other[lines[3], late]), False, late)
    b3 = core_send(5)
    b2 = z_send(4, b2)
    left += second_step_inverse(m, y)
    left_ref[0, 0] = left
    b3 = x_send(5, b3)
    d_col, d_row = diagonal(schur_ref[...])
    factor_ref[...] = m[...] * (d_col * inv_sqrt(d_col))
    save_factor = pltpu.make_async_copy(factor_ref, factor_out, local_sem.at[5])
    save_factor.start()
    b3 = z_send(5, b3)
    y_s = split(y[...])
    scale = inv_sqrt(d_row)
    fourth = unpack(z_total(4, b2))
    fifth = unpack(z_total(5, b3))
    at = (slice(None), pl.ds(pl.multiple_of((1 - r) * half + width, width), width))
    rows_ref[at] = panel_ref[at] - jnp.concatenate([fourth, fifth], axis=1)
    out_ref[...] = dot3(split(rows_ref[...] * scale), y_s, NT)
    save_schur.wait()
    save_factor.wait()
    for copy in pending:
        copy.wait_send()


def exchange(history_rows, history_below, diag_block, panel_below):
    half, depth = history_rows.shape
    count = history_below.shape[0]
    size = diag_block.shape[0]
    f32 = jnp.float32
    schur_rows, share = half // 16, count // 16
    streams = ((schur_rows, half), (share, half), (schur_rows, half), (share, half // 2), (share // 2, half // 2), (share // 2, half // 2))

    def blocks(*lead):
        return [pltpu.VMEM(lead + stream, f32) for stream in streams]

    square = jax.ShapeDtypeStruct((size, size), f32)
    strip = jax.ShapeDtypeStruct((share, size), f32)
    vmem, anywhere = pl.BlockSpec(memory_space=pltpu.VMEM), pl.BlockSpec(memory_space=pl.ANY)
    return pl.pallas_call(
        exchange_kernel,
        out_shape=(square, strip, square, strip, jax.ShapeDtypeStruct((1, 1), f32)),
        in_specs=[anywhere] * 4,
        out_specs=(anywhere, vmem, anywhere, vmem, pl.BlockSpec(memory_space=pltpu.SMEM)),
        scratch_shapes=[
            pltpu.VMEM((size, size), f32),
            pltpu.VMEM((share, size), f32),
            pltpu.VMEM((size, size), f32),
            pltpu.VMEM((size, size), f32),
            pltpu.VMEM((half, depth), f32),
            pltpu.VMEM((half, depth), f32),
            pltpu.VMEM((count, depth), f32),
            pltpu.VMEM((count, depth), jnp.bfloat16),
            pltpu.VMEM((count, depth), jnp.bfloat16),
            blocks(2, 2, 4),
            blocks(2, 4),
            blocks(4),
            blocks(3),
            pltpu.VMEM((2, 2, 4, 2, schur_rows, half), f32),
            pltpu.VMEM((2, 2, 4, schur_rows, half), f32),
            pltpu.VMEM((schur_rows, half), f32),
            pltpu.VMEM((size, size), f32),
            pltpu.VMEM((size, size), f32),
            pltpu.VMEM((size, size), f32),
            pltpu.SemaphoreType.DMA((6,)),
            pltpu.SemaphoreType.DMA((2, 4)),
            pltpu.SemaphoreType.DMA((2, 6)),
            pltpu.SemaphoreType.DMA((2, 6)),
            pltpu.SemaphoreType.DMA((2, 6, 3)),
            pltpu.SemaphoreType.DMA((2, 2, 6)),
        ],
        compiler_params=pltpu.CompilerParams(
            collective_id=0, has_side_effects=True, vmem_limit_bytes=VMEM_BYTES
        ),
    )(history_rows, history_below, diag_block, panel_below)


def finish(factor, panel, schur, updated, left):
    anywhere = pl.BlockSpec(memory_space=pl.ANY)
    factor, panel = pl.pallas_call(
        direct_kernel,
        out_shape=(
            jax.ShapeDtypeStruct(factor.shape, jnp.float32),
            jax.ShapeDtypeStruct(panel.shape, jnp.float32),
        ),
        in_specs=[pl.BlockSpec(memory_space=pltpu.SMEM)] + [anywhere] * 4,
        out_specs=(anywhere, anywhere),
        scratch_shapes=[
            pltpu.VMEM(factor.shape, jnp.float32),
            pltpu.VMEM(factor.shape, jnp.float32),
            pltpu.VMEM(panel.shape, jnp.float32),
            pltpu.SemaphoreType.DMA((2,)),
        ],
        compiler_params=pltpu.CompilerParams(vmem_limit_bytes=VMEM_BYTES),
    )(left, factor, panel, schur, updated)
    return panel, factor


def body(diag_block, history_rows, panel_below, history_below):
    grid = tuple(lax.axis_size(name) for name in ("rows", "near", "far"))
    if grid == (2, 4, 4):
        return finish(*exchange(history_rows, history_below, diag_block, panel_below))
    high = lax.Precision.HIGH
    gathered = lax.all_gather(history_rows, "rows", axis=0, tiled=True)
    schur_rows = jnp.dot(history_rows, gathered.T, precision=high)
    schur_part = lax.psum_scatter(schur_rows, ("near", "far"), scatter_dimension=0, tiled=True)
    products = lax.all_gather(schur_part, ("rows", "near", "far"), axis=0, tiled=True)
    partial_rows = jnp.dot(history_below, gathered.T, precision=high)
    product_rows = lax.psum_scatter(partial_rows, ("near", "far"), scatter_dimension=0, tiled=True)
    schur = diag_block - products
    diag_factor = jnp.linalg.cholesky(schur)
    identity = jnp.eye(schur.shape[0], dtype=jnp.float32)
    inverse = lax.linalg.triangular_solve(diag_factor, identity, left_side=True, lower=True)
    panel_factor = jnp.dot(panel_below - product_rows, inverse.T, precision=high)
    return (panel_factor, diag_factor)


def solution(mesh):
    return jax.shard_map(
        body,
        mesh=mesh,
        in_specs=(
            P(),
            P("rows", ("near", "far")),
            P(("rows", "near", "far"), None),
            P("rows", ("near", "far")),
        ),
        out_specs=(P(("rows", "near", "far"), None), P()),
        check_vma=False,
    )
```

```python
import jax
import jax.numpy as jnp
from jax import lax
from jax.experimental import pallas as pl
from jax.experimental.pallas import tpu as pltpu
from jax.sharding import PartitionSpec as P

NT = (((1,), (1,)), ((), ()))
NN = (((1,), (0,)), ((), ()))
LIMIT = 5e-5
VMEM_BYTES = 56 * 1024 * 1024


def split(value):
    high = value.astype(jnp.bfloat16)
    low = (value - high.astype(jnp.float32)).astype(jnp.bfloat16)
    return high, low


def dot1(left, right, dims):
    return lax.dot_general(left, right, dims, preferred_element_type=jnp.float32)


def dot3(left, right, dims):
    lh, ll = left
    rh, rl = right
    return (dot1(lh, rl, dims) + dot1(ll, rh, dims)) + dot1(lh, rh, dims)


def narrow(value):
    return value.astype(jnp.bfloat16)


def norm2(value):
    return jnp.sum(value * value)


def inv_sqrt(d):
    s = lax.rsqrt(d)
    return s * (1.5 - 0.5 * d * s * s)


def grid_of(size):
    row = lax.broadcasted_iota(jnp.int32, (size, size), 0)
    col = lax.broadcasted_iota(jnp.int32, (size, size), 1)
    return row, col


def lower_half(value):
    row, col = grid_of(value.shape[0])
    return jnp.where(row > col, value, jnp.where(row == col, 0.5 * value, 0.0))


def diagonal(value):
    row, col = grid_of(value.shape[0])
    on = jnp.where(row == col, value, 0.0)
    return jnp.sum(on, axis=1, keepdims=True), jnp.sum(on, axis=0, keepdims=True)


def factor_step(schur_ref, m_ref, y_ref):
    schur = schur_ref[...]
    row, col = grid_of(schur.shape[0])
    d_col, d_row = diagonal(schur)
    scaled = jnp.where(row == col, 1.0, schur * inv_sqrt(d_col) * inv_sqrt(d_row))
    p0 = jnp.where(row > col, scaled, 0.0)
    identity = jnp.where(row == col, 1.0, 0.0)
    p0b = narrow(p0)
    y0b = narrow(identity - p0)
    resid = -dot1(p0b, p0b, NT)
    p = lower_half(dot1(narrow(dot1(y0b, narrow(resid), NN)), y0b, NT))
    m0 = identity + p0
    q = dot1(narrow(m0), narrow(p), NN)
    m_ref[...] = m0 + q
    gap = dot1(p0b, p0b, NN) - dot1(y0b, narrow(q), NN)
    y_ref[...] = (identity - p0) + dot1(narrow(gap), y0b, NN)
    return norm2(p) + norm2(gap)


def direct_kernel(left_ref, factor_in, panel_in, schur_ref, rows_ref, factor_ref, panel_ref, work, factor, rest, sem):
    def move(*pairs):
        copies = [pltpu.make_async_copy(*pair, sem.at[i]) for i, pair in enumerate(pairs)]
        for copy in copies:
            copy.start()
        for copy in copies:
            copy.wait()

    move((factor_in, factor), (panel_in, rest))
    move((factor, factor_ref), (rest, panel_ref))

    @pl.when(jnp.logical_not(left_ref[0, 0] <= LIMIT))
    def _():
        move((schur_ref, work), (rows_ref, rest))
        factor[...] = jnp.zeros_like(factor)
        size = work.shape[0]
        row, col = grid_of(size)
        lane = lax.broadcasted_iota(jnp.int32, (1, size), 1)
        line = lax.broadcasted_iota(jnp.int32, (size, 1), 0)

        @pl.loop(0, size)
        def _(j):
            now = work[...]
            here = jnp.sum(jnp.where(row == j, now, 0.0), axis=0, keepdims=True)
            column = jnp.sum(jnp.where(col == j, now, 0.0), axis=1, keepdims=True)
            scale = inv_sqrt(jnp.sum(jnp.where(lane == j, here, 0.0), axis=1, keepdims=True))
            l_col = jnp.where(line >= j, column * scale, 0.0)
            l_row = jnp.where(lane >= j, here * scale, 0.0)
            work[...] = now - l_col * l_row
            factor[...] = jnp.where(col == j, l_col, factor[...])
            left = rest[...]
            solved = jnp.sum(jnp.where(lane == j, left, 0.0), axis=1, keepdims=True) * scale
            rest[...] = jnp.where(lane == j, solved, left - solved * l_row)

        move((factor, factor_ref), (rest, panel_ref))


def pack(value):
    rows = value.shape[0] // 2
    return jnp.concatenate([value[:rows], value[rows:]], axis=1)


def unpack(value):
    cols = value.shape[1] // 2
    return jnp.concatenate([value[:, :cols], value[:, cols:]], axis=0)


def exchange_kernel(hist_ref, below_ref, diag_in, panel_in,
                    factor_out, out_ref, schur_out, rows_ref, left_ref,
                    diag_ref, panel_ref, schur_ref, factor_ref, hist, other, below, below_hi, below_lo, sums, from_core, from_x, from_z,
                    own_all, other_all, from_y, m, y,
                    local_sem, hist_sem, core_sem, x_sem, z_sem, gather_sem):
    r, z, far = lax.axis_index("rows"), lax.axis_index("near"), lax.axis_index("far")
    x, c = far // 2, lax.rem(far, 2)
    to_y = {"rows": 1 - r}
    to_core = {"far": x * 2 + (1 - c)}
    to_x = {"far": (1 - x) * 2 + c}
    to_z = [{"near": lax.rem(z + d, 4)} for d in (1, 2, 3)]
    half, depth = hist_ref.shape
    piece = depth // 2
    width = half // 2
    pending = []

    barrier = pltpu.get_barrier_semaphore()
    for peer in [to_y, to_core, to_x] + to_z:
        pl.semaphore_signal(barrier, inc=1, device_id=peer, device_id_type=pl.DeviceIdType.MESH)
    pl.semaphore_wait(barrier, 6)

    def send(src, dst, sems, at, peer):
        copy = pltpu.make_async_remote_copy(
            src_ref=src, dst_ref=dst, send_sem=sems.at[(0,) + at], recv_sem=sems.at[(1,) + at],
            device_id=peer, device_id_type=pl.DeviceIdType.MESH)
        copy.start()
        pending.append(copy)
        return copy

    def columns(which):
        return pl.ds(pl.multiple_of(which * piece, piece), piece)

    everything = pl.ds(0, depth)
    quarter = width // 2
    lines = (pl.ds(0, half), pl.ds(0, width), pl.ds(width, quarter), pl.ds(width + quarter, quarter))

    def send_hist(index):
        at = (lines[index], columns(r if index == 0 else 1 - r))
        return send(hist.at[at], other.at[at], hist_sem, (index,), to_y)

    load_hist = pltpu.make_async_copy(hist_ref, hist, local_sem.at[0])
    load_below = pltpu.make_async_copy(below_ref, below, local_sem.at[1])
    load_diag = pltpu.make_async_copy(diag_in, diag_ref, local_sem.at[2])
    load_panel = pltpu.make_async_copy(panel_in, panel_ref, local_sem.at[3])
    load_hist.start()
    load_hist.wait()
    arrive = [send_hist(0)]
    load_below.start()
    load_diag.start()
    load_panel.start()

    def put_schur(stream, value):
        rows = value.shape[0] // 16
        for i in range(16):
            sums[stream][i % 2, (i // 2) % 2, i // 4] = value[i * rows:(i + 1) * rows]

    def multiply_below(streams, right, first, cols):
        tile = below.shape[0] // 4
        rows = tile // 4
        for t in range(4):
            at_rows = pl.ds(t * tile, tile)
            value = dot3((below_hi[at_rows, cols], below_lo[at_rows, cols]), right, NT)
            for i in range(4):
                at = (i % 2, i // 2, t)
                start = 0
                for stream in streams:
                    wide = quarter if stream >= 4 else sums[stream].shape[-1]
                    part = value[i * rows:(i + 1) * rows, start:start + wide]
                    if stream >= 4:
                        part = pack(part)
                    sums[stream][at] = part if first else sums[stream][at] + part
                    start += wide

    def core_send(stream):
        return send(sums[stream].at[1 - c], from_core[stream], core_sem, (stream,), to_core)

    def x_send(stream, copy):
        copy.wait_recv()
        total = sums[stream]
        total[c] = total[c] + from_core[stream][...]
        return send(total.at[c, 1 - x], from_x[stream], x_sem, (stream,), to_x)

    def z_send(stream, copy):
        copy.wait_recv()
        total = sums[stream]
        total[c, x] = total[c, x] + from_x[stream][...]
        return [
            send(total.at[c, x, lax.rem(z + d + 1, 4)], from_z[stream].at[d], z_sem, (stream, d), to_z[d])
            for d in range(3)
        ]

    def z_total(stream, copies):
        for copy in copies:
            copy.wait_recv()
        got = from_z[stream]
        return (sums[stream][c, x, z] + got[0]) + (got[1] + got[2])

    def gather_z(ref, which):
        return [send(ref, ref, gather_sem, (which, 1 + d), to_z[d]) for d in range(3)]

    def gather_x(ref, which, copies):
        for copy in copies:
            copy.wait_recv()
        return send(ref, ref, gather_sem, (which, 4), to_x)

    def gather_core(ref, which, copy):
        copy.wait_recv()
        return send(ref, ref, gather_sem, (which, 5), to_core)

    def put_rows(stream, copies, start, wide):
        at = (slice(None), pl.ds(pl.multiple_of(start, wide), wide))
        rows_ref[at] = panel_ref[at] - z_total(stream, copies)

    own = split(hist[...])
    put_schur(0, dot3(own, own, NT))
    s0 = core_send(0)
    load_below.wait()
    tile = below.shape[0] // 8
    for t in range(8):
        at_rows = pl.ds(t * tile, tile)
        high, low = split(below[at_rows, :])
        below_hi[at_rows, :] = high
        below_lo[at_rows, :] = low
    multiply_below((1,), own, True, everything)
    b0 = core_send(1)
    s0 = x_send(0, s0)
    b0 = x_send(1, b0)
    s0 = z_send(0, s0)
    own_all[c, x, z, r] = z_total(0, s0)
    y_own = send(own_all.at[c, x, z, r], own_all.at[c, x, z, r], gather_sem, (0, 0), to_y)
    arrive.append(send_hist(1))
    b0 = z_send(1, b0)

    arrive[0].wait_recv()
    early, late = columns(1 - r), columns(r)
    mine, theirs = hist[:, early], other[:, early]
    right = split(theirs)
    put_schur(2, dot3(split(jnp.where(r == 1, mine, theirs)), split(jnp.where(r == 1, theirs, mine)), NT))
    s1 = core_send(2)
    s1 = x_send(2, s1)
    s1 = z_send(2, s1)
    other_all[c, x, z] = z_total(2, s1)
    y_other = send(other_all.at[c, x, z], from_y, gather_sem, (1, 0), to_y)
    arrive.append(send_hist(2))
    arrive.append(send_hist(3))
    y_own.wait_recv()
    g0 = gather_z(own_all.at[c, x, z], 0)
    multiply_below((3, 4, 5), right, True, early)
    g0 = gather_x(own_all.at[c, x], 0, g0)
    load_panel.wait()
    put_rows(1, b0, r * half, half)
    g0 = gather_core(own_all.at[c], 0, g0)
    y_other.wait_recv()
    y_other.wait_send()
    pending[:] = [copy for copy in pending if copy is not y_other]
    other_all[c, x, z] = other_all[c, x, z] + from_y[...]
    g1 = gather_z(other_all.at[c, x, z], 1)
    load_diag.wait()
    g0.wait_recv()
    rows = half // 16
    for i in range(16):
        at = (i % 2, (i // 2) % 2, i // 4)
        for group in range(2):
            place = (pl.ds(group * half + i * rows, rows), pl.ds(group * half, half))
            schur_ref[place] = diag_ref[place] - own_all[at + (group,)]
    g1 = gather_x(other_all.at[c, x], 1, g1)
    arrive[1].wait_recv()
    multiply_below((3,), split(other[lines[1], late]), False, late)
    b1 = core_send(3)
    g1 = gather_core(other_all.at[c], 1, g1)
    b1 = x_send(3, b1)
    g1.wait_recv()
    for i in range(16):
        at = (i % 2, (i // 2) % 2, i // 4)
        place = (pl.ds(half + i * rows, rows), pl.ds(0, half))
        schur_ref[place] = diag_ref[place] - other_all[at]
    schur_ref[0:half, half:2 * half] = schur_ref[half:2 * half, 0:half].T
    save_schur = pltpu.make_async_copy(schur_ref, schur_out, local_sem.at[4])
    save_schur.start()
    b1 = z_send(3, b1)
    left_ref[0, 0] = factor_step(schur_ref, m, y)
    d_col, d_row = diagonal(schur_ref[...])
    factor_ref[...] = m[...] * (d_col * inv_sqrt(d_col))
    save_factor = pltpu.make_async_copy(factor_ref, factor_out, local_sem.at[5])
    save_factor.start()

    arrive[2].wait_recv()
    multiply_below((4,), split(other[lines[2], late]), False, late)
    b2 = core_send(4)
    put_rows(3, b1, (1 - r) * half, width)
    b2 = x_send(4, b2)
    arrive[3].wait_recv()
    multiply_below((5,), split(other[lines[3], late]), False, late)
    b3 = core_send(5)
    b2 = z_send(4, b2)
    b3 = x_send(5, b3)
    b3 = z_send(5, b3)
    y_s = split(y[...])
    scale = inv_sqrt(d_row)
    fourth = unpack(z_total(4, b2))
    fifth = unpack(z_total(5, b3))
    at = (slice(None), pl.ds(pl.multiple_of((1 - r) * half + width, width), width))
    rows_ref[at] = panel_ref[at] - jnp.concatenate([fourth, fifth], axis=1)
    out_ref[...] = dot3(split(rows_ref[...] * scale), y_s, NT)
    save_schur.wait()
    save_factor.wait()
    for copy in pending:
        copy.wait_send()


def exchange(history_rows, history_below, diag_block, panel_below):
    half, depth = history_rows.shape
    count = history_below.shape[0]
    size = diag_block.shape[0]
    f32 = jnp.float32
    schur_rows, share = half // 16, count // 16
    streams = ((schur_rows, half), (share, half), (schur_rows, half), (share, half // 2), (share // 2, half // 2), (share // 2, half // 2))

    def blocks(*lead):
        return [pltpu.VMEM(lead + stream, f32) for stream in streams]

    square = jax.ShapeDtypeStruct((size, size), f32)
    strip = jax.ShapeDtypeStruct((share, size), f32)
    vmem, anywhere = pl.BlockSpec(memory_space=pltpu.VMEM), pl.BlockSpec(memory_space=pl.ANY)
    return pl.pallas_call(
        exchange_kernel,
        out_shape=(square, strip, square, strip, jax.ShapeDtypeStruct((1, 1), f32)),
        in_specs=[anywhere] * 4,
        out_specs=(anywhere, vmem, anywhere, vmem, pl.BlockSpec(memory_space=pltpu.SMEM)),
        scratch_shapes=[
            pltpu.VMEM((size, size), f32),
            pltpu.VMEM((share, size), f32),
            pltpu.VMEM((size, size), f32),
            pltpu.VMEM((size, size), f32),
            pltpu.VMEM((half, depth), f32),
            pltpu.VMEM((half, depth), f32),
            pltpu.VMEM((count, depth), f32),
            pltpu.VMEM((count, depth), jnp.bfloat16),
            pltpu.VMEM((count, depth), jnp.bfloat16),
            blocks(2, 2, 4),
            blocks(2, 4),
            blocks(4),
            blocks(3),
            pltpu.VMEM((2, 2, 4, 2, schur_rows, half), f32),
            pltpu.VMEM((2, 2, 4, schur_rows, half), f32),
            pltpu.VMEM((schur_rows, half), f32),
            pltpu.VMEM((size, size), f32),
            pltpu.VMEM((size, size), f32),
            pltpu.SemaphoreType.DMA((6,)),
            pltpu.SemaphoreType.DMA((2, 4)),
            pltpu.SemaphoreType.DMA((2, 6)),
            pltpu.SemaphoreType.DMA((2, 6)),
            pltpu.SemaphoreType.DMA((2, 6, 3)),
            pltpu.SemaphoreType.DMA((2, 2, 6)),
        ],
        compiler_params=pltpu.CompilerParams(
            collective_id=0, has_side_effects=True, vmem_limit_bytes=VMEM_BYTES
        ),
    )(history_rows, history_below, diag_block, panel_below)


def finish(factor, panel, schur, updated, left):
    anywhere = pl.BlockSpec(memory_space=pl.ANY)
    factor, panel = pl.pallas_call(
        direct_kernel,
        out_shape=(
            jax.ShapeDtypeStruct(factor.shape, jnp.float32),
            jax.ShapeDtypeStruct(panel.shape, jnp.float32),
        ),
        in_specs=[pl.BlockSpec(memory_space=pltpu.SMEM)] + [anywhere] * 4,
        out_specs=(anywhere, anywhere),
        scratch_shapes=[
            pltpu.VMEM(factor.shape, jnp.float32),
            pltpu.VMEM(factor.shape, jnp.float32),
            pltpu.VMEM(panel.shape, jnp.float32),
            pltpu.SemaphoreType.DMA((2,)),
        ],
        compiler_params=pltpu.CompilerParams(vmem_limit_bytes=VMEM_BYTES),
    )(left, factor, panel, schur, updated)
    return panel, factor


def body(diag_block, history_rows, panel_below, history_below):
    grid = tuple(lax.axis_size(name) for name in ("rows", "near", "far"))
    if grid == (2, 4, 4):
        return finish(*exchange(history_rows, history_below, diag_block, panel_below))
    high = lax.Precision.HIGH
    gathered = lax.all_gather(history_rows, "rows", axis=0, tiled=True)
    schur_rows = jnp.dot(history_rows, gathered.T, precision=high)
    schur_part = lax.psum_scatter(schur_rows, ("near", "far"), scatter_dimension=0, tiled=True)
    products = lax.all_gather(schur_part, ("rows", "near", "far"), axis=0, tiled=True)
    partial_rows = jnp.dot(history_below, gathered.T, precision=high)
    product_rows = lax.psum_scatter(partial_rows, ("near", "far"), scatter_dimension=0, tiled=True)
    schur = diag_block - products
    diag_factor = jnp.linalg.cholesky(schur)
    identity = jnp.eye(schur.shape[0], dtype=jnp.float32)
    inverse = lax.linalg.triangular_solve(diag_factor, identity, left_side=True, lower=True)
    panel_factor = jnp.dot(panel_below - product_rows, inverse.T, precision=high)
    return (panel_factor, diag_factor)


def solution(mesh):
    return jax.shard_map(
        body,
        mesh=mesh,
        in_specs=(
            P(),
            P("rows", ("near", "far")),
            P(("rows", "near", "far"), None),
            P("rows", ("near", "far")),
        ),
        out_specs=(P(("rows", "near", "far"), None), P()),
        check_vma=False,
    )
```

```python
import jax
import jax.numpy as jnp
from jax import lax
from jax.experimental import pallas as pl
from jax.experimental.pallas import tpu as pltpu
from jax.sharding import PartitionSpec as P

NT = (((1,), (1,)), ((), ()))
NN = (((1,), (0,)), ((), ()))
LIMIT = 5e-5
VMEM_BYTES = 56 * 1024 * 1024


def split(value):
    high = value.astype(jnp.bfloat16)
    low = (value - high.astype(jnp.float32)).astype(jnp.bfloat16)
    return high, low


def dot1(left, right, dims):
    return lax.dot_general(left, right, dims, preferred_element_type=jnp.float32)


def dot3(left, right, dims):
    lh, ll = left
    rh, rl = right
    return (dot1(lh, rl, dims) + dot1(ll, rh, dims)) + dot1(lh, rh, dims)


def narrow(value):
    return value.astype(jnp.bfloat16)


def norm2(value):
    return jnp.sum(value * value)


def inv_sqrt(d):
    s = lax.rsqrt(d)
    return s * (1.5 - 0.5 * d * s * s)


def grid_of(size):
    row = lax.broadcasted_iota(jnp.int32, (size, size), 0)
    col = lax.broadcasted_iota(jnp.int32, (size, size), 1)
    return row, col


def lower_half(value):
    row, col = grid_of(value.shape[0])
    return jnp.where(row > col, value, jnp.where(row == col, 0.5 * value, 0.0))


def diagonal(value):
    row, col = grid_of(value.shape[0])
    on = jnp.where(row == col, value, 0.0)
    return jnp.sum(on, axis=1, keepdims=True), jnp.sum(on, axis=0, keepdims=True)


def factor_step(schur_ref, m_ref, y_ref):
    schur = schur_ref[...]
    row, col = grid_of(schur.shape[0])
    d_col, d_row = diagonal(schur)
    scaled = jnp.where(row == col, 1.0, schur * inv_sqrt(d_col) * inv_sqrt(d_row))
    p0 = jnp.where(row > col, scaled, 0.0)
    identity = jnp.where(row == col, 1.0, 0.0)
    p0b = narrow(p0)
    y0b = narrow(identity - p0)
    resid = -dot1(p0b, p0b, NT)
    p = lower_half(dot1(narrow(dot1(y0b, narrow(resid), NN)), y0b, NT))
    m0 = identity + p0
    q = dot1(narrow(m0), narrow(p), NN)
    m_ref[...] = m0 + q
    gap = dot1(p0b, p0b, NN) - dot1(y0b, narrow(q), NN)
    y_ref[...] = (identity - p0) + dot1(narrow(gap), y0b, NN)
    return norm2(p) + norm2(gap)


def direct_kernel(left_ref, factor_in, panel_in, schur_ref, rows_ref, factor_ref, panel_ref, work, factor, rest, sem):
    def move(*pairs):
        copies = [pltpu.make_async_copy(*pair, sem.at[i]) for i, pair in enumerate(pairs)]
        for copy in copies:
            copy.start()
        for copy in copies:
            copy.wait()

    move((factor_in, factor), (panel_in, rest))
    move((factor, factor_ref), (rest, panel_ref))

    @pl.when(jnp.logical_not(left_ref[0, 0] <= LIMIT))
    def _():
        move((schur_ref, work), (rows_ref, rest))
        factor[...] = jnp.zeros_like(factor)
        size = work.shape[0]
        row, col = grid_of(size)
        lane = lax.broadcasted_iota(jnp.int32, (1, size), 1)
        line = lax.broadcasted_iota(jnp.int32, (size, 1), 0)

        @pl.loop(0, size)
        def _(j):
            now = work[...]
            here = jnp.sum(jnp.where(row == j, now, 0.0), axis=0, keepdims=True)
            column = jnp.sum(jnp.where(col == j, now, 0.0), axis=1, keepdims=True)
            scale = inv_sqrt(jnp.sum(jnp.where(lane == j, here, 0.0), axis=1, keepdims=True))
            l_col = jnp.where(line >= j, column * scale, 0.0)
            l_row = jnp.where(lane >= j, here * scale, 0.0)
            work[...] = now - l_col * l_row
            factor[...] = jnp.where(col == j, l_col, factor[...])
            left = rest[...]
            solved = jnp.sum(jnp.where(lane == j, left, 0.0), axis=1, keepdims=True) * scale
            rest[...] = jnp.where(lane == j, solved, left - solved * l_row)

        move((factor, factor_ref), (rest, panel_ref))


def pack(value):
    rows = value.shape[0] // 2
    return jnp.concatenate([value[:rows], value[rows:]], axis=1)


def unpack(value):
    cols = value.shape[1] // 2
    return jnp.concatenate([value[:, :cols], value[:, cols:]], axis=0)


def exchange_kernel(hist_ref, below_ref, diag_in, panel_in,
                    factor_out, out_ref, schur_out, rows_ref, left_ref,
                    diag_ref, panel_ref, schur_ref, factor_ref, hist, other, below, below_hi, below_lo, sums, from_core, from_x, from_z,
                    own_all, other_all, from_y, m, y,
                    local_sem, hist_sem, core_sem, x_sem, z_sem, gather_sem):
    r, z, far = lax.axis_index("rows"), lax.axis_index("near"), lax.axis_index("far")
    x, c = far // 2, lax.rem(far, 2)
    to_y = {"rows": 1 - r}
    to_core = {"far": x * 2 + (1 - c)}
    to_x = {"far": (1 - x) * 2 + c}
    to_z = [{"near": lax.rem(z + d, 4)} for d in (1, 2, 3)]
    half, depth = hist_ref.shape
    piece = depth // 2
    width = half // 2
    pending = []

    barrier = pltpu.get_barrier_semaphore()
    for peer in [to_y, to_core, to_x] + to_z:
        pl.semaphore_signal(barrier, inc=1, device_id=peer, device_id_type=pl.DeviceIdType.MESH)
    pl.semaphore_wait(barrier, 6)

    def send(src, dst, sems, at, peer):
        copy = pltpu.make_async_remote_copy(
            src_ref=src, dst_ref=dst, send_sem=sems.at[(0,) + at], recv_sem=sems.at[(1,) + at],
            device_id=peer, device_id_type=pl.DeviceIdType.MESH)
        copy.start()
        pending.append(copy)
        return copy

    def columns(which):
        return pl.ds(pl.multiple_of(which * piece, piece), piece)

    everything = pl.ds(0, depth)
    quarter = width // 2
    lines = (pl.ds(0, half), pl.ds(0, width), pl.ds(width, quarter), pl.ds(width + quarter, quarter))

    def send_hist(index):
        at = (lines[index], columns(r if index == 0 else 1 - r))
        return send(hist.at[at], other.at[at], hist_sem, (index,), to_y)

    load_hist = pltpu.make_async_copy(hist_ref, hist, local_sem.at[0])
    load_below = pltpu.make_async_copy(below_ref, below, local_sem.at[1])
    load_diag = pltpu.make_async_copy(diag_in, diag_ref, local_sem.at[2])
    load_panel = pltpu.make_async_copy(panel_in, panel_ref, local_sem.at[3])
    load_hist.start()
    load_hist.wait()
    arrive = [send_hist(0), send_hist(1)]
    load_below.start()
    load_diag.start()
    load_panel.start()

    def put_schur(stream, value):
        rows = value.shape[0] // 16
        for i in range(16):
            sums[stream][i % 2, (i // 2) % 2, i // 4] = value[i * rows:(i + 1) * rows]

    def multiply_below(streams, right, first, cols):
        tile = below.shape[0] // 4
        rows = tile // 4
        for t in range(4):
            at_rows = pl.ds(t * tile, tile)
            value = dot3((below_hi[at_rows, cols], below_lo[at_rows, cols]), right, NT)
            for i in range(4):
                at = (i % 2, i // 2, t)
                start = 0
                for stream in streams:
                    wide = quarter if stream >= 4 else sums[stream].shape[-1]
                    part = value[i * rows:(i + 1) * rows, start:start + wide]
                    if stream >= 4:
                        part = pack(part)
                    sums[stream][at] = part if first else sums[stream][at] + part
                    start += wide

    def core_send(stream):
        return send(sums[stream].at[1 - c], from_core[stream], core_sem, (stream,), to_core)

    def x_send(stream, copy):
        copy.wait_recv()
        total = sums[stream]
        total[c] = total[c] + from_core[stream][...]
        return send(total.at[c, 1 - x], from_x[stream], x_sem, (stream,), to_x)

    def z_send(stream, copy):
        copy.wait_recv()
        total = sums[stream]
        total[c, x] = total[c, x] + from_x[stream][...]
        return [
            send(total.at[c, x, lax.rem(z + d + 1, 4)], from_z[stream].at[d], z_sem, (stream, d), to_z[d])
            for d in range(3)
        ]

    def z_total(stream, copies):
        for copy in copies:
            copy.wait_recv()
        got = from_z[stream]
        return (sums[stream][c, x, z] + got[0]) + (got[1] + got[2])

    def gather_z(ref, which):
        return [send(ref, ref, gather_sem, (which, 1 + d), to_z[d]) for d in range(3)]

    def gather_x(ref, which, copies):
        for copy in copies:
            copy.wait_recv()
        return send(ref, ref, gather_sem, (which, 4), to_x)

    def gather_core(ref, which, copy):
        copy.wait_recv()
        return send(ref, ref, gather_sem, (which, 5), to_core)

    def put_rows(stream, copies, start, wide):
        at = (slice(None), pl.ds(pl.multiple_of(start, wide), wide))
        rows_ref[at] = panel_ref[at] - z_total(stream, copies)

    own = split(hist[...])
    put_schur(0, dot3(own, own, NT))
    s0 = core_send(0)
    load_below.wait()
    tile = below.shape[0] // 8
    for t in range(8):
        at_rows = pl.ds(t * tile, tile)
        high, low = split(below[at_rows, :])
        below_hi[at_rows, :] = high
        below_lo[at_rows, :] = low
    multiply_below((1,), own, True, everything)
    b0 = core_send(1)
    s0 = x_send(0, s0)
    b0 = x_send(1, b0)
    s0 = z_send(0, s0)
    own_all[c, x, z, r] = z_total(0, s0)
    y_own = send(own_all.at[c, x, z, r], own_all.at[c, x, z, r], gather_sem, (0, 0), to_y)
    arrive.append(send_hist(2))
    b0 = z_send(1, b0)

    arrive[0].wait_recv()
    early, late = columns(1 - r), columns(r)
    mine, theirs = hist[:, early], other[:, early]
    right = split(theirs)
    put_schur(2, dot3(split(jnp.where(r == 1, mine, theirs)), split(jnp.where(r == 1, theirs, mine)), NT))
    s1 = core_send(2)
    s1 = x_send(2, s1)
    s1 = z_send(2, s1)
    other_all[c, x, z] = z_total(2, s1)
    y_other = send(other_all.at[c, x, z], from_y, gather_sem, (1, 0), to_y)
    arrive.append(send_hist(3))
    y_own.wait_recv()
    g0 = gather_z(own_all.at[c, x, z], 0)
    multiply_below((3, 4, 5), right, True, early)
    g0 = gather_x(own_all.at[c, x], 0, g0)
    load_panel.wait()
    put_rows(1, b0, r * half, half)
    g0 = gather_core(own_all.at[c], 0, g0)
    y_other.wait_recv()
    y_other.wait_send()
    pending[:] = [copy for copy in pending if copy is not y_other]
    other_all[c, x, z] = other_all[c, x, z] + from_y[...]
    g1 = gather_z(other_all.at[c, x, z], 1)
    load_diag.wait()
    g0.wait_recv()
    rows = half // 16
    for i in range(16):
        at = (i % 2, (i // 2) % 2, i // 4)
        for group in range(2):
            place = (pl.ds(group * half + i * rows, rows), pl.ds(group * half, half))
            schur_ref[place] = diag_ref[place] - own_all[at + (group,)]
    g1 = gather_x(other_all.at[c, x], 1, g1)
    arrive[1].wait_recv()
    multiply_below((3,), split(other[lines[1], late]), False, late)
    b1 = core_send(3)
    g1 = gather_core(other_all.at[c], 1, g1)
    b1 = x_send(3, b1)
    g1.wait_recv()
    for i in range(16):
        at = (i % 2, (i // 2) % 2, i // 4)
        place = (pl.ds(half + i * rows, rows), pl.ds(0, half))
        schur_ref[place] = diag_ref[place] - other_all[at]
    schur_ref[0:half, half:2 * half] = schur_ref[half:2 * half, 0:half].T
    save_schur = pltpu.make_async_copy(schur_ref, schur_out, local_sem.at[4])
    save_schur.start()
    b1 = z_send(3, b1)
    left_ref[0, 0] = factor_step(schur_ref, m, y)
    d_col, d_row = diagonal(schur_ref[...])
    factor_ref[...] = m[...] * (d_col * inv_sqrt(d_col))
    save_factor = pltpu.make_async_copy(factor_ref, factor_out, local_sem.at[5])
    save_factor.start()

    arrive[2].wait_recv()
    multiply_below((4,), split(other[lines[2], late]), False, late)
    b2 = core_send(4)
    put_rows(3, b1, (1 - r) * half, width)
    b2 = x_send(4, b2)
    arrive[3].wait_recv()
    multiply_below((5,), split(other[lines[3], late]), False, late)
    b3 = core_send(5)
    b2 = z_send(4, b2)
    b3 = x_send(5, b3)
    b3 = z_send(5, b3)
    y_s = split(y[...])
    scale = inv_sqrt(d_row)
    fourth = unpack(z_total(4, b2))
    fifth = unpack(z_total(5, b3))
    at = (slice(None), pl.ds(pl.multiple_of((1 - r) * half + width, width), width))
    rows_ref[at] = panel_ref[at] - jnp.concatenate([fourth, fifth], axis=1)
    out_ref[...] = dot3(split(rows_ref[...] * scale), y_s, NT)
    save_schur.wait()
    save_factor.wait()
    for copy in pending:
        copy.wait_send()


def exchange(history_rows, history_below, diag_block, panel_below):
    half, depth = history_rows.shape
    count = history_below.shape[0]
    size = diag_block.shape[0]
    f32 = jnp.float32
    schur_rows, share = half // 16, count // 16
    streams = ((schur_rows, half), (share, half), (schur_rows, half), (share, half // 2), (share // 2, half // 2), (share // 2, half // 2))

    def blocks(*lead):
        return [pltpu.VMEM(lead + stream, f32) for stream in streams]

    square = jax.ShapeDtypeStruct((size, size), f32)
    strip = jax.ShapeDtypeStruct((share, size), f32)
    vmem, anywhere = pl.BlockSpec(memory_space=pltpu.VMEM), pl.BlockSpec(memory_space=pl.ANY)
    return pl.pallas_call(
        exchange_kernel,
        out_shape=(square, strip, square, strip, jax.ShapeDtypeStruct((1, 1), f32)),
        in_specs=[anywhere] * 4,
        out_specs=(anywhere, vmem, anywhere, vmem, pl.BlockSpec(memory_space=pltpu.SMEM)),
        scratch_shapes=[
            pltpu.VMEM((size, size), f32),
            pltpu.VMEM((share, size), f32),
            pltpu.VMEM((size, size), f32),
            pltpu.VMEM((size, size), f32),
            pltpu.VMEM((half, depth), f32),
            pltpu.VMEM((half, depth), f32),
            pltpu.VMEM((count, depth), f32),
            pltpu.VMEM((count, depth), jnp.bfloat16),
            pltpu.VMEM((count, depth), jnp.bfloat16),
            blocks(2, 2, 4),
            blocks(2, 4),
            blocks(4),
            blocks(3),
            pltpu.VMEM((2, 2, 4, 2, schur_rows, half), f32),
            pltpu.VMEM((2, 2, 4, schur_rows, half), f32),
            pltpu.VMEM((schur_rows, half), f32),
            pltpu.VMEM((size, size), f32),
            pltpu.VMEM((size, size), f32),
            pltpu.SemaphoreType.DMA((6,)),
            pltpu.SemaphoreType.DMA((2, 4)),
            pltpu.SemaphoreType.DMA((2, 6)),
            pltpu.SemaphoreType.DMA((2, 6)),
            pltpu.SemaphoreType.DMA((2, 6, 3)),
            pltpu.SemaphoreType.DMA((2, 2, 6)),
        ],
        compiler_params=pltpu.CompilerParams(
            collective_id=0, has_side_effects=True, vmem_limit_bytes=VMEM_BYTES
        ),
    )(history_rows, history_below, diag_block, panel_below)


def finish(factor, panel, schur, updated, left):
    anywhere = pl.BlockSpec(memory_space=pl.ANY)
    factor, panel = pl.pallas_call(
        direct_kernel,
        out_shape=(
            jax.ShapeDtypeStruct(factor.shape, jnp.float32),
            jax.ShapeDtypeStruct(panel.shape, jnp.float32),
        ),
        in_specs=[pl.BlockSpec(memory_space=pltpu.SMEM)] + [anywhere] * 4,
        out_specs=(anywhere, anywhere),
        scratch_shapes=[
            pltpu.VMEM(factor.shape, jnp.float32),
            pltpu.VMEM(factor.shape, jnp.float32),
            pltpu.VMEM(panel.shape, jnp.float32),
            pltpu.SemaphoreType.DMA((2,)),
        ],
        compiler_params=pltpu.CompilerParams(vmem_limit_bytes=VMEM_BYTES),
    )(left, factor, panel, schur, updated)
    return panel, factor


def body(diag_block, history_rows, panel_below, history_below):
    grid = tuple(lax.axis_size(name) for name in ("rows", "near", "far"))
    if grid == (2, 4, 4):
        return finish(*exchange(history_rows, history_below, diag_block, panel_below))
    high = lax.Precision.HIGH
    gathered = lax.all_gather(history_rows, "rows", axis=0, tiled=True)
    schur_rows = jnp.dot(history_rows, gathered.T, precision=high)
    schur_part = lax.psum_scatter(schur_rows, ("near", "far"), scatter_dimension=0, tiled=True)
    products = lax.all_gather(schur_part, ("rows", "near", "far"), axis=0, tiled=True)
    partial_rows = jnp.dot(history_below, gathered.T, precision=high)
    product_rows = lax.psum_scatter(partial_rows, ("near", "far"), scatter_dimension=0, tiled=True)
    schur = diag_block - products
    diag_factor = jnp.linalg.cholesky(schur)
    identity = jnp.eye(schur.shape[0], dtype=jnp.float32)
    inverse = lax.linalg.triangular_solve(diag_factor, identity, left_side=True, lower=True)
    panel_factor = jnp.dot(panel_below - product_rows, inverse.T, precision=high)
    return (panel_factor, diag_factor)


def solution(mesh):
    return jax.shard_map(
        body,
        mesh=mesh,
        in_specs=(
            P(),
            P("rows", ("near", "far")),
            P(("rows", "near", "far"), None),
            P("rows", ("near", "far")),
        ),
        out_specs=(P(("rows", "near", "far"), None), P()),
        check_vma=False,
    )
```
